32 devices in a mesh: groups: 2 (over y), section: 4 (over z), dp: 2 (over x), sub: 2 (over core).
Axes of the slice: x: 2, y: 2, z: 4, core: 2. Of those that a mesh axis runs over, the one named last changes fastest.
Arguments:
- inputs: bfloat16 [16, 128, 4096], P(('groups', 'section', 'dp'), None, 'sub'), parts along dimension 0, may hold values from -6 to 6
- queries: bfloat16 [16, 128, 4096], P(('groups', 'section', 'dp'), None, 'sub'), parts along dimension 0, may hold values from -210 to 210
- out_grad: bfloat16 [16, 128, 4096], P(('groups', 'section', 'dp'), None, 'sub'), parts along dimension 0, may hold values from -6 to 6
- lengths: int32 [16], P(('groups', 'section', 'dp')), parts along dimension 0, may hold values from 32 to 128, as said below
- key_matrix: bfloat16 [4096, 512], P('section', 'sub'), may hold values from -0.09375 to 0.09375
- value_matrix: bfloat16 [4096, 512], P('section', 'sub'), may hold values from -0.09375 to 0.09375
Outputs:
- query_grad: bfloat16 [16, 128, 4096], P(('groups', 'section', 'dp'), None, 'sub'), parts along dimension 0
- input_grad: bfloat16 [16, 128, 4096], P(('groups', 'section', 'dp'), None, 'sub'), parts along dimension 0
- key_weight_grad: float32 [8192, 512], P(('groups', 'section'), 'sub'), parts along dimension 0
- value_weight_grad: float32 [8192, 512], P(('groups', 'section'), 'sub'), parts along dimension 0
The draws below stay inside these ranges and needn't reach their ends.
There are 2 independent parts, one for each index of `groups`. The reference program is written for one: setup_inputs(seed, part) draws one part's arguments, and reference() takes and returns one part's arrays. A program takes and returns all parts, laid end to end along the dimension named above; an argument that names none is the same for every part. Nothing has to cross between parts.
Inputs may be any that keep to these rules, and one draw needn't show every extreme that they name: `lengths`: keys at or past a micro-batch's length are excluded; some micro-batch has all 128 tokens valid.
All inputs are finite; a program needn't handle non-finite values.
Results may differ from the reference program's by a relative error of at most 0.011.
The reference program's roundings to bfloat16 on the way count: a program that leaves them out, or rounds other values in their place, can miss the bound.
Values may be sent and summed in bfloat16 or wider, within the bound.
A program may use at most 64 MiB of HBM per device.

```python
import math
import jax
import jax.numpy as jnp
from jax import lax

MODEL_FEATURES = 4096
KEY_VALUE_HEADS = 4
HEAD_SIZE = 128
QUERY_GROUP = 8
BATCH_TOKENS = 128
QH = 32
MICRO_BATCHES = 8


def draw_queries(key, part):
    key = jax.random.fold_in(key, 7)
    base_key = jax.random.fold_in(key, 0)
    complete_shape = (MICRO_BATCHES, BATCH_TOKENS, QUERY_GROUP * KEY_VALUE_HEADS * HEAD_SIZE)
    entries = jax.random.truncated_normal(base_key, -6.0, 6.0, complete_shape, jnp.float32)
    return entries.astype(jnp.bfloat16)


def draw_lengths(key, part):
    key = jax.random.fold_in(key, 11)
    length_key, place_key = jax.random.split(key)
    drawn = jax.random.randint(length_key, (MICRO_BATCHES,), BATCH_TOKENS // 4, BATCH_TOKENS + 1, jnp.int32)
    full_index = jax.random.randint(place_key, (), 0, MICRO_BATCHES, jnp.int32)
    return jnp.where(jnp.arange(MICRO_BATCHES, dtype=jnp.int32) == full_index, BATCH_TOKENS, drawn).astype(jnp.int32)


def spiked(array, stream_key, source, target, shards_of, factor):
    def block_of(axis_at):
        return (jnp.arange(array.shape[axis_at]) // (array.shape[axis_at] // shards_of)).reshape((-1,) + (1,) * (array.ndim - 1 - axis_at))

    near = jax.random.permutation(stream_key, shards_of)[block_of(target)]
    far = (block_of(target) + shards_of // 2) % shards_of
    return jnp.where((block_of(source) == near) | (block_of(source) == far), factor * array, array)


def block_levels(key, extent, cuts, low, high):
    loudness, own = 1.0, jax.random.fold_in(key, 6)
    for position, parts in cuts:
        heights = jnp.exp(jax.random.uniform(jax.random.fold_in(own, position), (parts,), jnp.float32, low / len(cuts), high / len(cuts)))
        loudness = loudness * jnp.repeat(heights, extent[position] // parts).reshape([-1 if axis == position else 1 for axis in range(len(extent))])
    return loudness


def scatter_about(key, extent, spread, limit, shards=(), kind=jnp.bfloat16):
    values = jax.random.normal(key, extent, jnp.float32) * spread
    if len(shards) > 0:
        values = block_levels(key, extent, shards, -0.22, 0.18) * values
    return jnp.clip(values, min=-limit, max=limit).astype(kind)


def noise_with(key, dims, width, reach, shards, heavy, kind=jnp.bfloat16):
    values = width * jax.random.normal(key, dims, jnp.float32)
    if shards:
        values = values * block_levels(key, dims, shards, -0.22, 0.18)
    return jnp.clip(spiked(values, jax.random.fold_in(key, 3), *heavy), -reach, reach).astype(kind)


def setup_inputs(seed: int = 0, part: int = 0) -> dict:
    streams_of = jax.random.split(jax.random.key(seed), 7)
    part_keys = jax.random.split(jax.random.fold_in(streams_of[6], part), 7)
    inputs = noise_with(part_keys[0], (MICRO_BATCHES, BATCH_TOKENS, MODEL_FEATURES), 1.0, 6.0, ((0, 8), (2, 2)), (0, 2, 8, 2.0))
    queries = draw_queries(jax.random.fold_in(jax.random.fold_in(streams_of[6], part), 71), part)
    out_grad = scatter_about(part_keys[2], (MICRO_BATCHES, BATCH_TOKENS, QH * HEAD_SIZE), 1.0, 6.0, ((0, 8), (2, 2)))
    lengths = draw_lengths(jax.random.fold_in(jax.random.fold_in(streams_of[6], part), 71), part)
    key_matrix = scatter_about(streams_of[4], (MODEL_FEATURES, KEY_VALUE_HEADS * HEAD_SIZE), MODEL_FEATURES ** -0.5, 0.09375, ((0, 4), (1, 2)))
    value_matrix = scatter_about(streams_of[5], (MODEL_FEATURES, KEY_VALUE_HEADS * HEAD_SIZE), MODEL_FEATURES ** -0.5, 0.09375, ((0, 4), (1, 2)))
    return {"inputs": inputs, "queries": queries, "out_grad": out_grad, "lengths": lengths, "key_matrix": key_matrix, "value_matrix": value_matrix}


def rotary_tables(positions_total, head_width):
    positions = jnp.arange(positions_total, dtype=jnp.float32)[:, None]
    frequency = jnp.exp(jnp.arange(head_width // 2, dtype=jnp.float32) * (-2.0 * math.log(10000.0) / head_width))
    angles = positions * frequency[None, :]
    return jnp.cos(angles)[:, None, :], jnp.sin(angles)[:, None, :]


def apply_rotary(tensor, cosine_table, sine_values_table):
    half_width = tensor.shape[-1] // 2
    leading = tensor[..., :half_width]
    trailing = tensor[..., half_width:]
    return jnp.concatenate([leading * cosine_table - trailing * sine_values_table, trailing * cosine_table + leading * sine_values_table], axis=-1)


def unrotate(tensor, cosine_table, sine_values_table):
    half_width = tensor.shape[-1] // 2
    leading = tensor[..., :half_width]
    trailing = tensor[..., half_width:]
    return jnp.concatenate([leading * cosine_table + trailing * sine_values_table, trailing * cosine_table - leading * sine_values_table], axis=-1)


def reference(inputs, queries, out_grad, lengths, key_matrix, value_matrix):
    score_scale = HEAD_SIZE ** -0.5
    head_columns = KEY_VALUE_HEADS * HEAD_SIZE
    joined = jnp.concatenate([key_matrix, value_matrix], axis=1)

    def per_batch(packed):
        token_rows, query_matrix_rows, gradient_rows, valid_length = packed
        linear_key = jnp.dot(token_rows, key_matrix, preferred_element_type=jnp.float32)
        value_rows = jnp.dot(token_rows, value_matrix, preferred_element_type=jnp.float32).astype(jnp.bfloat16)
        cosine_table, sine_values_table = rotary_tables(BATCH_TOKENS, HEAD_SIZE)
        rotary_output = apply_rotary(linear_key.reshape(BATCH_TOKENS, KEY_VALUE_HEADS, HEAD_SIZE), cosine_table, sine_values_table).astype(jnp.bfloat16)
        heads_of_value = value_rows.reshape(BATCH_TOKENS, KEY_VALUE_HEADS, HEAD_SIZE).astype(jnp.float32)
        key_heads = rotary_output.astype(jnp.float32)
        grouped_query = query_matrix_rows.reshape(BATCH_TOKENS, KEY_VALUE_HEADS, QUERY_GROUP, HEAD_SIZE).astype(jnp.float32)
        grouped_gradient = gradient_rows.reshape(BATCH_TOKENS, KEY_VALUE_HEADS, QUERY_GROUP, HEAD_SIZE).astype(jnp.float32)
        scores = jnp.einsum('tkgd,ukd->kgtu', grouped_query, key_heads) * score_scale
        row_ids = jnp.arange(BATCH_TOKENS, dtype=jnp.int32)[:, None]
        col_ids = jnp.arange(BATCH_TOKENS, dtype=jnp.int32)[None, :]
        allowed = (col_ids <= row_ids) & (col_ids < valid_length)
        scores = jnp.where(allowed, scores, -1e30)
        row_peak = jnp.max(scores, axis=-1, keepdims=True)
        exponent = jnp.exp(scores - row_peak)
        soft_weights = exponent / jnp.sum(exponent, axis=-1, keepdims=True)
        soft_rounded = soft_weights.astype(jnp.bfloat16).astype(jnp.float32)
        prob_grad = jnp.einsum('tkgd,ukd->kgtu', grouped_gradient, heads_of_value)
        centre = jnp.sum(soft_weights * prob_grad, axis=-1, keepdims=True)
        logit_grad = (soft_weights * (prob_grad - centre) * score_scale).astype(jnp.bfloat16).astype(jnp.float32)
        query_grad = jnp.einsum('kgtu,ukd->tkgd', logit_grad, key_heads).astype(jnp.bfloat16).reshape(BATCH_TOKENS, QH * HEAD_SIZE)
        key_grad_rotated = jnp.einsum('kgtu,tkgd->ukd', logit_grad, grouped_query)
        value_grad = jnp.einsum('kgtu,tkgd->ukd', soft_rounded, grouped_gradient)
        key_grad = unrotate(key_grad_rotated, cosine_table, sine_values_table)
        proj_grads = jnp.concatenate([key_grad.reshape(BATCH_TOKENS, head_columns), value_grad.reshape(BATCH_TOKENS, head_columns)], axis=1).astype(jnp.bfloat16)
        input_grad = lax.dot_general(proj_grads, joined, (((1,), (1,)), ((), ())), preferred_element_type=jnp.float32).astype(jnp.bfloat16)
        return query_grad, input_grad, proj_grads

    query_grad, input_grad, proj_grads = lax.map(per_batch, (inputs, queries, out_grad, lengths))
    flat_inputs = inputs.reshape(MICRO_BATCHES * BATCH_TOKENS, MODEL_FEATURES)
    flat_grads = proj_grads.reshape(MICRO_BATCHES * BATCH_TOKENS, 2 * head_columns)
    weight_grads = lax.dot_general(flat_inputs, flat_grads, (((0,), (0,)), ((), ())), preferred_element_type=jnp.float32) / MICRO_BATCHES
    return query_grad, input_grad, weight_grads[:, :head_columns], weight_grads[:, head_columns:]
```

```python
import functools
import math

import jax
import jax.numpy as jnp
import numpy as np
from jax import lax
from jax.experimental import pallas as pl
from jax.experimental.pallas import tpu as pltpu
from jax.sharding import PartitionSpec as P

HEAD_SIZE = 128
QUERY_GROUP = 8
BF16 = jnp.bfloat16
F32 = jnp.float32


def rotary_tables(positions_total):
    half = HEAD_SIZE // 2
    frequency = np.exp(np.arange(half) * (-2.0 * math.log(10000.0) / HEAD_SIZE))
    angles = np.arange(positions_total)[:, None] * frequency[None, :]
    cos, sin = np.cos(angles), np.sin(angles)
    return (
        np.concatenate([cos, cos], axis=1).astype(np.float32),
        np.concatenate([-sin, sin], axis=1).astype(np.float32),
    )


def repeat(start, stop, body):
    if stop - start <= 4:
        for i in range(start, stop):
            body(i)
    else:

        def step(i, carry):
            body(i)
            return carry

        lax.fori_loop(start, stop, step, 0)


def dot_nt(a, b):
    return lax.dot_general(a, b, (((1,), (1,)), ((), ())), preferred_element_type=F32)


def dot_tn(a, b):
    return lax.dot_general(a, b, (((0,), (0,)), ((), ())), preferred_element_type=F32)


def dot_nn(a, b):
    return jnp.dot(a, b, preferred_element_type=F32)


def swap_halves(a):
    half = HEAD_SIZE // 2
    return jnp.concatenate([a[:, half:], a[:, :half]], axis=1)


def kernel(
    G, S, D,
    len_ref, x_ref, q_ref, og_ref, k_ref, v_ref, cos_ref, sin_ref,
    qg_ref, ig_ref, kw_ref, vw_ref,
    wbuf, xbuf, xg, pgg, igs, igr,
    zw_s, zw_r, xw_s, xw_r, yw_s, yw_r, ax_s, ax_r, by_s, by_r,
    xs_s, xs_r, zx_s, zx_r, xx_s, xx_r, cx_s, cx_r,
    zp_s, zp_r, xp_s, xp_r, ig_s, ig_r,
):
    g, s, d, c = (lax.axis_index(a) for a in ("groups", "section", "dp", "sub"))
    T = x_ref.shape[1]
    C = k_ref.shape[1]
    R = k_ref.shape[0]
    H = S // 2
    rq = R // (G * D)
    th = T // 2
    kv = C // HEAD_SIZE
    score_scale = HEAD_SIZE ** (-0.5)

    def other_s(k):
        return lax.rem(s + k, S)

    def other_d(k):
        return lax.rem(d + k, D)

    def other_g(k):
        return lax.rem(g + k, G)

    sibling = {"sub": 1 - c}

    def rows_of(gg, dd):
        return pl.ds(pl.multiple_of((gg * D + dd) * rq, rq), rq)

    my_tokens = pl.ds(pl.multiple_of(c * th, th), th)

    def remote(src, dst, send, recv, device):
        return pltpu.make_async_remote_copy(
            src_ref=src, dst_ref=dst, send_sem=send, recv_sem=recv,
            device_id=device, device_id_type=pl.DeviceIdType.MESH,
        )

    def w_z(to, block):
        part = wbuf.at[block, rows_of(g, d)]
        return remote(part, part, zw_s.at[to], zw_r.at[block], {"section": to})

    def w_x(to, block, dd):
        part = wbuf.at[block, rows_of(g, dd)]
        return remote(part, part, xw_s.at[block, to], xw_r.at[block, dd], {"dp": to})

    def w_y(to, block, gg):
        part = wbuf.at[block, rows_of(gg, d)]
        return remote(part, part, yw_s.at[block, to], yw_r.at[block, gg], {"groups": to})

    def w_ax(to, block, gg, dd):
        part = wbuf.at[block, rows_of(gg, dd), pl.ds(0, C)]
        return remote(part, part, ax_s.at[block, gg, to], ax_r.at[block, gg, dd], {"dp": to})

    def w_by(to, block, gg, dd):
        part = wbuf.at[block, rows_of(gg, dd), pl.ds(C, C)]
        return remote(part, part, by_s.at[block, to, dd], by_r.at[block, gg, dd], {"groups": to})

    def x_sub(cc):
        part = xbuf.at[pl.ds(cc * H, H)]
        return remote(part, part, xs_s.at[0], xs_r.at[0], sibling)

    def x_z(to, owner):
        src = xbuf.at[to, my_tokens]
        dst = xg.at[owner, d, my_tokens]
        return remote(src, dst, zx_s.at[to], zx_r.at[owner], {"section": to})

    def x_x(to, block, dd):
        part = xg.at[block, dd, my_tokens]
        return remote(part, part, xx_s.at[block, to], xx_r.at[block, dd], {"dp": to})

    def x_c(cc):
        part = xg.at[:, :, pl.ds(pl.multiple_of(cc * th, th), th)]
        return remote(part, part, cx_s.at[0], cx_r.at[0], sibling)

    def p_z(to, owner):
        part = pgg.at[owner, d]
        return remote(part, part, zp_s.at[to], zp_r.at[owner], {"section": to})

    def p_x(to, block, dd):
        part = pgg.at[block, dd]
        return remote(part, part, xp_s.at[block, to], xp_r.at[block, dd], {"dp": to})

    def i_c(i):
        return remote(igs.at[i], igr.at[i], ig_s.at[i], ig_r.at[i], sibling)

    barrier = pltpu.get_barrier_semaphore()

    def greet(device):
        pl.semaphore_signal(
            barrier, inc=1, device_id=device, device_id_type=pl.DeviceIdType.MESH
        )

    greet(sibling)
    repeat(1, S, lambda k: greet({"section": other_s(k)}))
    repeat(1, D, lambda k: greet({"dp": other_d(k)}))
    repeat(1, G, lambda k: greet({"groups": other_g(k)}))
    wbuf[s, :, :C] = k_ref[...]
    wbuf[s, :, C:] = v_ref[...]
    for i in range(H):
        xbuf[c * H + i] = x_ref[0, :, i * R : (i + 1) * R]
    pl.semaphore_wait(barrier, 1 + (S - 1) + (D - 1) + (G - 1))

    x_sub(c).start()
    repeat(1, S, lambda k: w_z(other_s(k), s).start())
    x_sub(1 - c).wait_recv()
    repeat(1, S, lambda k: x_z(other_s(k), s).start())
    xg[s, d, my_tokens] = xbuf[s, my_tokens]

    def first_hand(k):
        block = other_s(k)
        w_z(block, block).wait_recv()
        repeat(1, G, lambda j: w_y(other_g(j), block, g).start())
        repeat(1, D, lambda j: w_x(other_d(j), block, d).start())

    repeat(1, S, first_hand)
    projected = dot_nn(xbuf[s], wbuf[s])

    def second_hand(k):
        block = other_s(k)

        def from_y(j):
            gg = other_g(j)
            w_y(gg, block, gg).wait_recv()
            repeat(1, D, lambda i: w_ax(other_d(i), block, gg, d).start())

        def from_x(j):
            dd = other_d(j)
            w_x(dd, block, dd).wait_recv()
            repeat(1, G, lambda i: w_by(other_g(i), block, g, dd).start())

        repeat(1, G, from_y)
        repeat(1, D, from_x)

    repeat(1, S, second_hand)

    repeat(1, D, lambda j: x_x(other_d(j), s, d).start())

    def inputs_on(k):
        block = other_s(k)
        x_z(block, block).wait_recv()
        repeat(1, D, lambda j: x_x(other_d(j), block, d).start())

    repeat(1, S, inputs_on)

    def project(k, total):
        block = other_s(k)

        def diagonal(j):
            gg = other_g(j)

            def part(i):
                dd = other_d(i)
                w_ax(dd, block, gg, dd).wait_recv()
                w_by(gg, block, gg, dd).wait_recv()

            repeat(1, D, part)

        repeat(1, G, diagonal)
        return total + dot_nn(xbuf[block], wbuf[block])

    if S <= 4:
        for k in range(1, S):
            projected = project(k, projected)
    else:
        projected = lax.fori_loop(1, S, project, projected)

    cos, sin = cos_ref[...], sin_ref[...]
    length = len_ref[0]
    u_ids = lax.broadcasted_iota(jnp.int32, (T, T), 0)
    t_ids = lax.broadcasted_iota(jnp.int32, (T, T), 1)
    allowed = (u_ids <= t_ids) & (u_ids < length)
    for h in range(kv):
        linear = projected[:, h * HEAD_SIZE : (h + 1) * HEAD_SIZE]
        keys = (linear * cos + swap_halves(linear) * sin).astype(BF16)
        values = projected[:, C + h * HEAD_SIZE : C + (h + 1) * HEAD_SIZE].astype(BF16)
        key_grad = jnp.zeros((T, HEAD_SIZE), F32)
        value_grad = jnp.zeros((T, HEAD_SIZE), F32)
        for j in range(QUERY_GROUP):
            at = slice((h * QUERY_GROUP + j) * HEAD_SIZE, (h * QUERY_GROUP + j + 1) * HEAD_SIZE)
            query, grad = q_ref[0, :, at], og_ref[0, :, at]
            scores = jnp.where(allowed, dot_nt(keys, query) * score_scale, -1e30)
            exponent = jnp.exp(scores - jnp.max(scores, axis=0, keepdims=True))
            probs = exponent / jnp.sum(exponent, axis=0, keepdims=True)
            prob_grad = dot_nt(values, grad)
            centre = jnp.sum(probs * prob_grad, axis=0, keepdims=True)
            logit_grad = (probs * (prob_grad - centre) * score_scale).astype(BF16)
            qg_ref[0, :, at] = dot_tn(logit_grad, keys).astype(BF16)
            key_grad += dot_nn(logit_grad, query)
            value_grad += dot_nn(probs.astype(BF16), grad)
        key_grad = key_grad * cos - swap_halves(key_grad) * sin
        pgg[s, d, :, h * HEAD_SIZE : (h + 1) * HEAD_SIZE] = key_grad.astype(BF16)
        pgg[s, d, :, C + h * HEAD_SIZE : C + (h + 1) * HEAD_SIZE] = value_grad.astype(BF16)

    repeat(1, S, lambda k: p_z(other_s(k), s).start())
    repeat(1, D, lambda j: p_x(other_d(j), s, d).start())
    proj_grads = pgg[s, d]
    for i in range(H):
        igs[i] = dot_nt(proj_grads, wbuf[(1 - c) * H + i])
        i_c(i).start()

    def grads_on(k):
        block = other_s(k)
        p_z(block, block).wait_recv()
        repeat(1, D, lambda j: p_x(other_d(j), block, d).start())

    repeat(1, S, grads_on)

    def inputs_in(block):
        def part(j):
            dd = other_d(j)
            x_x(dd, block, dd).wait_recv()

        repeat(1, D, part)

    repeat(0, S, inputs_in)
    x_c(c).start()
    for i in range(H):
        own = dot_nt(proj_grads, wbuf[c * H + i])
        i_c(i).wait_recv()
        ig_ref[0, :, i * R : (i + 1) * R] = (own + igr[i]).astype(BF16)

    x_c(1 - c).wait_recv()

    def grads_in(block):
        def part(j):
            dd = other_d(j)
            p_x(dd, block, dd).wait_recv()

        repeat(1, D, part)

    repeat(0, S, grads_in)

    mean = 1.0 / (S * D)
    tile = min(R, 256)
    per = D if D * T <= 512 else 1

    def weight_sum(lo, hi, first):
        for r in range(0, R, tile):
            xs = xg[lo:hi, :, :, r : r + tile].reshape((hi - lo) * D * T, tile)
            ps = pgg[lo:hi].reshape((hi - lo) * D * T, 2 * C)
            part = dot_tn(xs, ps) * mean
            kw_ref[r : r + tile] = part[:, :C]
            vw_ref[r : r + tile] = part[:, C:]

    if S * D * T <= 1024:
        weight_sum(0, S, True)
    else:
        kw_ref[...] = jnp.zeros_like(kw_ref)
        vw_ref[...] = jnp.zeros_like(vw_ref)

        def add_batch(b, carry):
            part = dot_tn(xg[b // D, lax.rem(b, D)], pgg[b // D, lax.rem(b, D)]) * mean
            kw_ref[...] += part[:, :C]
            vw_ref[...] += part[:, C:]
            return carry

        lax.fori_loop(0, S * D, add_batch, 0)

    x_sub(c).wait_send()
    x_c(c).wait_send()
    for i in range(H):
        i_c(i).wait_send()
    repeat(1, D, lambda j: x_x(other_d(j), s, d).wait_send())
    repeat(1, D, lambda j: p_x(other_d(j), s, d).wait_send())

    def sent(k):
        block = other_s(k)
        w_z(block, s).wait_send()
        x_z(block, s).wait_send()
        p_z(block, s).wait_send()

        def along_y(j):
            gg = other_g(j)
            w_y(gg, block, g).wait_send()

            def both(i):
                dd = other_d(i)
                w_ax(dd, block, gg, d).wait_send()
                w_by(gg, block, g, dd).wait_send()

            repeat(1, D, both)

        def along_x(j):
            dd = other_d(j)
            w_x(dd, block, d).wait_send()
            x_x(dd, block, d).wait_send()
            p_x(dd, block, d).wait_send()

        repeat(1, G, along_y)
        repeat(1, D, along_x)

    repeat(1, S, sent)


def shards(G, S, D, inputs, queries, out_grad, lengths, key_matrix, value_matrix):
    T = inputs.shape[1]
    R, C = key_matrix.shape
    H = S // 2
    cos, sin = rotary_tables(T)
    dma = pltpu.SemaphoreType.DMA
    vmem = pl.BlockSpec(memory_space=pltpu.VMEM)
    pairs = lambda *shape: [dma(shape), dma(shape)]
    return pl.pallas_call(
        functools.partial(kernel, G, S, D),
        out_shape=(
            jax.ShapeDtypeStruct(queries.shape, BF16),
            jax.ShapeDtypeStruct(inputs.shape, BF16),
            jax.ShapeDtypeStruct((R, C), F32),
            jax.ShapeDtypeStruct((R, C), F32),
        ),
        in_specs=[pl.BlockSpec(memory_space=pltpu.SMEM)] + [vmem] * 7,
        out_specs=(vmem,) * 4,
        scratch_shapes=[
            pltpu.VMEM((S, R, 2 * C), BF16),
            pltpu.VMEM((S, T, R), BF16),
            pltpu.VMEM((S, D, T, R), BF16),
            pltpu.VMEM((S, D, T, 2 * C), BF16),
            pltpu.VMEM((H, T, R), F32),
            pltpu.VMEM((H, T, R), F32),
            *pairs(S), *pairs(S, D), *pairs(S, G), *pairs(S, G, D), *pairs(S, G, D),
            *pairs(1), *pairs(S), *pairs(S, D), *pairs(1),
            *pairs(S), *pairs(S, D), *pairs(H),
        ],
        compiler_params=pltpu.CompilerParams(
            collective_id=0, has_side_effects=True, vmem_limit_bytes=56 * 2**20
        ),
    )(lengths, inputs, queries, out_grad, key_matrix, value_matrix, jnp.asarray(cos), jnp.asarray(sin))


def solution(mesh):
    sizes = (mesh.shape["groups"], mesh.shape["section"], mesh.shape["dp"])
    batch = P(("groups", "section", "dp"), None, "sub")
    weights = P("section", "sub")
    rows = P(("groups", "section"), "sub")
    return jax.shard_map(
        functools.partial(shards, *sizes),
        mesh=mesh,
        in_specs=(batch, batch, batch, P(("groups", "section", "dp")), weights, weights),
        out_specs=(batch, batch, rows, rows),
        check_vma=False,
    )
```

```python
import functools
import math

import jax
import jax.numpy as jnp
import numpy as np
from jax import lax
from jax.experimental import pallas as pl
from jax.experimental.pallas import tpu as pltpu
from jax.sharding import PartitionSpec as P

HEAD_SIZE = 128
QUERY_GROUP = 8
BF16 = jnp.bfloat16
F32 = jnp.float32


def rotary_tables(positions_total):
    half = HEAD_SIZE // 2
    frequency = np.exp(np.arange(half) * (-2.0 * math.log(10000.0) / HEAD_SIZE))
    angles = np.arange(positions_total)[:, None] * frequency[None, :]
    cos, sin = np.cos(angles), np.sin(angles)
    return (
        np.concatenate([cos, cos], axis=1).astype(np.float32),
        np.concatenate([-sin, sin], axis=1).astype(np.float32),
    )


def repeat(start, stop, body):
    if stop - start <= 4:
        for i in range(start, stop):
            body(i)
    else:

        def step(i, carry):
            body(i)
            return carry

        lax.fori_loop(start, stop, step, 0)


def dot_nt(a, b):
    return lax.dot_general(a, b, (((1,), (1,)), ((), ())), preferred_element_type=F32)


def dot_tn(a, b):
    return lax.dot_general(a, b, (((0,), (0,)), ((), ())), preferred_element_type=F32)


def dot_nn(a, b):
    return jnp.dot(a, b, preferred_element_type=F32)


def swap_halves(a):
    half = HEAD_SIZE // 2
    return jnp.concatenate([a[:, half:], a[:, :half]], axis=1)


def kernel(
    G, S, D,
    len_ref, x_ref, q_ref, og_ref, k_ref, v_ref, cos_ref, sin_ref,
    qg_ref, ig_ref, kw_ref, vw_ref,
    wbuf, xbuf, xg, pgg, igs, igr, projected,
    zw_s, zw_r, xw_s, xw_r, yw_s, yw_r, ax_s, ax_r, by_s, by_r,
    xs_s, xs_r, zx_s, zx_r, xx_s, xx_r, cx_s, cx_r,
    zp_s, zp_r, xp_s, xp_r, ig_s, ig_r,
):
    g, s, d, c = (lax.axis_index(a) for a in ("groups", "section", "dp", "sub"))
    T = x_ref.shape[1]
    C = k_ref.shape[1]
    R = k_ref.shape[0]
    H = S // 2
    rq = R // (G * D)
    th = T // 2
    kv = C // HEAD_SIZE
    score_scale = HEAD_SIZE ** (-0.5)

    def other_s(k):
        return lax.rem(s + k, S)

    def other_d(k):
        return lax.rem(d + k, D)

    def other_g(k):
        return lax.rem(g + k, G)

    sibling = {"sub": 1 - c}

    def rows_of(gg, dd):
        return pl.ds(pl.multiple_of((gg * D + dd) * rq, rq), rq)

    my_tokens = pl.ds(pl.multiple_of(c * th, th), th)

    def remote(src, dst, send, recv, device):
        return pltpu.make_async_remote_copy(
            src_ref=src, dst_ref=dst, send_sem=send, recv_sem=recv,
            device_id=device, device_id_type=pl.DeviceIdType.MESH,
        )

    def half_of(half):
        return pl.ds(half * C, C)

    def w_z(to, way, block, half):
        part = wbuf.at[block, rows_of(g, d), half_of(half)]
        return remote(part, part, zw_s.at[way, block, half], zw_r.at[block, half], {"section": to})

    def w_x(to, block, dd, half):
        part = wbuf.at[block, rows_of(g, dd), half_of(half)]
        return remote(part, part, xw_s.at[block, to, half], xw_r.at[block, dd, half], {"dp": to})

    def w_y(to, block, gg, half):
        part = wbuf.at[block, rows_of(gg, d), half_of(half)]
        return remote(part, part, yw_s.at[block, to, half], yw_r.at[block, gg, half], {"groups": to})

    def w_ax(to, block, gg, dd):
        part = wbuf.at[block, rows_of(gg, dd), half_of(0)]
        return remote(part, part, ax_s.at[block, gg, to], ax_r.at[block, gg, dd], {"dp": to})

    def w_by(to, block, gg, dd):
        part = wbuf.at[block, rows_of(gg, dd), half_of(1)]
        return remote(part, part, by_s.at[block, to, dd], by_r.at[block, gg, dd], {"groups": to})

    def x_sub(cc):
        part = xbuf.at[pl.ds(cc * H, H)]
        return remote(part, part, xs_s.at[0], xs_r.at[0], sibling)

    def x_z(to, owner):
        src = xbuf.at[to, my_tokens]
        dst = xg.at[owner, d, my_tokens]
        return remote(src, dst, zx_s.at[to], zx_r.at[owner], {"section": to})

    def x_x(to, block, dd):
        part = xg.at[block, dd, my_tokens]
        return remote(part, part, xx_s.at[block, to], xx_r.at[block, dd], {"dp": to})

    def x_c(cc):
        part = xg.at[:, :, pl.ds(pl.multiple_of(cc * th, th), th)]
        return remote(part, part, cx_s.at[0], cx_r.at[0], sibling)

    def p_z(to, way, owner):
        part = pgg.at[owner, d]
        return remote(part, part, zp_s.at[way, owner], zp_r.at[owner], {"section": to})

    def p_x(to, block, dd):
        part = pgg.at[block, dd]
        return remote(part, part, xp_s.at[block, to], xp_r.at[block, dd], {"dp": to})

    def i_c(i):
        return remote(igs.at[i], igr.at[i], ig_s.at[i], ig_r.at[i], sibling)

    barrier = pltpu.get_barrier_semaphore()

    def greet(device):
        pl.semaphore_signal(
            barrier, inc=1, device_id=device, device_id_type=pl.DeviceIdType.MESH
        )

    greet(sibling)
    repeat(1, S, lambda k: greet({"section": other_s(k)}))
    repeat(1, D, lambda k: greet({"dp": other_d(k)}))
    repeat(1, G, lambda k: greet({"groups": other_g(k)}))
    wbuf[s, :, :C] = k_ref[...]
    wbuf[s, :, C:] = v_ref[...]
    for i in range(H):
        xbuf[c * H + i] = x_ref[0, :, i * R : (i + 1) * R]
    pl.semaphore_wait(barrier, 1 + (S - 1) + (D - 1) + (G - 1))

    def along_line(k, body):
        @pl.when(s >= k)
        def _():
            body(s - k, 0, s < S - 1, s + 1)

        @pl.when(s + k < S)
        def _():
            body(s + k, 1, s > 0, s - 1)

    def both_ways(body):
        @pl.when(s < S - 1)
        def _():
            body(s + 1, 0)

        @pl.when(s > 0)
        def _():
            body(s - 1, 1)

    x_sub(c).start()
    for half in range(2):
        both_ways(lambda to, way: w_z(to, way, s, half).start())
    x_sub(1 - c).wait_recv()
    xg[s, d, my_tokens] = xbuf[s, my_tokens]
    projected[...] = dot_nn(xbuf[s], wbuf[s])

    def first_hand(block, way, more, to):
        for half in range(2):
            w_z(s, way, block, half).wait_recv()

            @pl.when(more)
            def _():
                w_z(to, way, block, half).start()

            repeat(1, G, lambda j: w_y(other_g(j), block, g, half).start())
            repeat(1, D, lambda j: w_x(other_d(j), block, d, half).start())

    def second_hand(block, way, more, to):
        for half in range(2):

            def from_y(j):
                gg = other_g(j)
                w_y(gg, block, gg, half).wait_recv()
                if half == 0:
                    repeat(1, D, lambda i: w_ax(other_d(i), block, gg, d).start())

            def from_x(j):
                dd = other_d(j)
                w_x(dd, block, dd, half).wait_recv()
                if half == 1:
                    repeat(1, G, lambda i: w_by(other_g(i), block, g, dd).start())

            repeat(1, G, from_y)
            repeat(1, D, from_x)

    def project(block, way, more, to):
        def diagonal(j):
            gg = other_g(j)

            def part(i):
                dd = other_d(i)
                w_ax(dd, block, gg, dd).wait_recv()
                w_by(gg, block, gg, dd).wait_recv()

            repeat(1, D, part)

        repeat(1, G, diagonal)
        projected[...] += dot_nn(xbuf[block], wbuf[block])

    along_line(1, first_hand)

    def hop(k):
        along_line(k, first_hand)
        along_line(k - 1, second_hand)

    repeat(2, S, hop)
    repeat(1, S, lambda k: x_z(other_s(k), s).start())
    along_line(S - 1, second_hand)
    repeat(1, D, lambda j: x_x(other_d(j), s, d).start())
    repeat(1, S, lambda k: along_line(k, project))

    def inputs_on(k):
        block = other_s(k)
        x_z(block, block).wait_recv()
        repeat(1, D, lambda j: x_x(other_d(j), block, d).start())

    repeat(1, S, inputs_on)

    cos, sin = cos_ref[...], sin_ref[...]
    length = len_ref[0]
    u_ids = lax.broadcasted_iota(jnp.int32, (T, T), 0)
    t_ids = lax.broadcasted_iota(jnp.int32, (T, T), 1)
    allowed = (u_ids <= t_ids) & (u_ids < length)
    for h in range(kv):
        linear = projected[:, h * HEAD_SIZE : (h + 1) * HEAD_SIZE]
        keys = (linear * cos + swap_halves(linear) * sin).astype(BF16)
        values = projected[:, C + h * HEAD_SIZE : C + (h + 1) * HEAD_SIZE].astype(BF16)
        key_grad = jnp.zeros((T, HEAD_SIZE), F32)
        value_grad = jnp.zeros((T, HEAD_SIZE), F32)
        for j in range(QUERY_GROUP):
            at = slice((h * QUERY_GROUP + j) * HEAD_SIZE, (h * QUERY_GROUP + j + 1) * HEAD_SIZE)
            query, grad = q_ref[0, :, at], og_ref[0, :, at]
            scores = jnp.where(allowed, dot_nt(keys, query) * score_scale, -1e30)
            exponent = jnp.exp(scores - jnp.max(scores, axis=0, keepdims=True))
            probs = exponent / jnp.sum(exponent, axis=0, keepdims=True)
            prob_grad = dot_nt(values, grad)
            centre = jnp.sum(probs * prob_grad, axis=0, keepdims=True)
            logit_grad = (probs * (prob_grad - centre) * score_scale).astype(BF16)
            qg_ref[0, :, at] = dot_tn(logit_grad, keys).astype(BF16)
            key_grad += dot_nn(logit_grad, query)
            value_grad += dot_nn(probs.astype(BF16), grad)
        key_grad = key_grad * cos - swap_halves(key_grad) * sin
        pgg[s, d, :, h * HEAD_SIZE : (h + 1) * HEAD_SIZE] = key_grad.astype(BF16)
        pgg[s, d, :, C + h * HEAD_SIZE : C + (h + 1) * HEAD_SIZE] = value_grad.astype(BF16)

    both_ways(lambda to, way: p_z(to, way, s).start())
    repeat(1, D, lambda j: p_x(other_d(j), s, d).start())
    proj_grads = pgg[s, d]
    for i in range(H):
        igs[i] = dot_nt(proj_grads, wbuf[(1 - c) * H + i])
        i_c(i).start()

    def grads_on(block, way, more, to):
        p_z(s, way, block).wait_recv()

        @pl.when(more)
        def _():
            p_z(to, way, block).start()

        repeat(1, D, lambda j: p_x(other_d(j), block, d).start())

    repeat(1, S, lambda k: along_line(k, grads_on))

    def inputs_in(block):
        def part(j):
            dd = other_d(j)
            x_x(dd, block, dd).wait_recv()

        repeat(1, D, part)

    repeat(0, S, inputs_in)
    x_c(c).start()
    for i in range(H):
        own = dot_nt(proj_grads, wbuf[c * H + i])
        i_c(i).wait_recv()
        ig_ref[0, :, i * R : (i + 1) * R] = (own + igr[i]).astype(BF16)

    x_c(1 - c).wait_recv()

    def grads_in(block):
        def part(j):
            dd = other_d(j)
            p_x(dd, block, dd).wait_recv()

        repeat(1, D, part)

    repeat(0, S, grads_in)

    mean = 1.0 / (S * D)
    tile = min(R, 256)
    per = D if D * T <= 512 else 1

    def weight_sum(lo, hi, first):
        for r in range(0, R, tile):
            xs = xg[lo:hi, :, :, r : r + tile].reshape((hi - lo) * D * T, tile)
            ps = pgg[lo:hi].reshape((hi - lo) * D * T, 2 * C)
            part = dot_tn(xs, ps) * mean
            kw_ref[r : r + tile] = part[:, :C]
            vw_ref[r : r + tile] = part[:, C:]

    if S * D * T <= 1024:
        weight_sum(0, S, True)
    else:
        kw_ref[...] = jnp.zeros_like(kw_ref)
        vw_ref[...] = jnp.zeros_like(vw_ref)

        def add_batch(b, carry):
            part = dot_tn(xg[b // D, lax.rem(b, D)], pgg[b // D, lax.rem(b, D)]) * mean
            kw_ref[...] += part[:, :C]
            vw_ref[...] += part[:, C:]
            return carry

        lax.fori_loop(0, S * D, add_batch, 0)

    x_sub(c).wait_send()
    x_c(c).wait_send()
    for i in range(H):
        i_c(i).wait_send()
    repeat(1, D, lambda j: x_x(other_d(j), s, d).wait_send())
    repeat(1, D, lambda j: p_x(other_d(j), s, d).wait_send())

    def line_sent(to, way, block):
        for half in range(2):
            w_z(to, way, block, half).wait_send()
        p_z(to, way, block).wait_send()

    both_ways(lambda to, way: line_sent(to, way, s))

    def sent(block, way, more, to):
        @pl.when(more)
        def _():
            line_sent(to, way, block)

        x_z(block, s).wait_send()

        def along_y(j):
            gg = other_g(j)
            for half in range(2):
                w_y(gg, block, g, half).wait_send()

            def both(i):
                dd = other_d(i)
                w_ax(dd, block, gg, d).wait_send()
                w_by(gg, block, g, dd).wait_send()

            repeat(1, D, both)

        def along_x(j):
            dd = other_d(j)
            for half in range(2):
                w_x(dd, block, d, half).wait_send()
            x_x(dd, block, d).wait_send()
            p_x(dd, block, d).wait_send()

        repeat(1, G, along_y)
        repeat(1, D, along_x)

    repeat(1, S, lambda k: along_line(k, sent))


def shards(G, S, D, inputs, queries, out_grad, lengths, key_matrix, value_matrix):
    T = inputs.shape[1]
    R, C = key_matrix.shape
    H = S // 2
    cos, sin = rotary_tables(T)
    dma = pltpu.SemaphoreType.DMA
    vmem = pl.BlockSpec(memory_space=pltpu.VMEM)
    pairs = lambda *shape: [dma(shape), dma(shape)]
    return pl.pallas_call(
        functools.partial(kernel, G, S, D),
        out_shape=(
            jax.ShapeDtypeStruct(queries.shape, BF16),
            jax.ShapeDtypeStruct(inputs.shape, BF16),
            jax.ShapeDtypeStruct((R, C), F32),
            jax.ShapeDtypeStruct((R, C), F32),
        ),
        in_specs=[pl.BlockSpec(memory_space=pltpu.SMEM)] + [vmem] * 7,
        out_specs=(vmem,) * 4,
        scratch_shapes=[
            pltpu.VMEM((S, R, 2 * C), BF16),
            pltpu.VMEM((S, T, R), BF16),
            pltpu.VMEM((S, D, T, R), BF16),
            pltpu.VMEM((S, D, T, 2 * C), BF16),
            pltpu.VMEM((H, T, R), F32),
            pltpu.VMEM((H, T, R), F32),
            pltpu.VMEM((T, 2 * C), F32),
            dma((2, S, 2)), dma((S, 2)), *pairs(S, D, 2), *pairs(S, G, 2), *pairs(S, G, D), *pairs(S, G, D),
            *pairs(1), *pairs(S), *pairs(S, D), *pairs(1),
            dma((2, S)), dma((S,)), *pairs(S, D), *pairs(H),
        ],
        compiler_params=pltpu.CompilerParams(
            collective_id=0, has_side_effects=True, vmem_limit_bytes=56 * 2**20
        ),
    )(lengths, inputs, queries, out_grad, key_matrix, value_matrix, jnp.asarray(cos), jnp.asarray(sin))


def solution(mesh):
    sizes = (mesh.shape["groups"], mesh.shape["section"], mesh.shape["dp"])
    batch = P(("groups", "section", "dp"), None, "sub")
    weights = P("section", "sub")
    rows = P(("groups", "section"), "sub")
    return jax.shard_map(
        functools.partial(shards, *sizes),
        mesh=mesh,
        in_specs=(batch, batch, batch, P(("groups", "section", "dp")), weights, weights),
        out_specs=(batch, batch, rows, rows),
        check_vma=False,
    )
```

```python
import functools
import math

import jax
import jax.numpy as jnp
import numpy as np
from jax import lax
from jax.experimental import pallas as pl
from jax.experimental.pallas import tpu as pltpu
from jax.sharding import PartitionSpec as P

HEAD_SIZE = 128
QUERY_GROUP = 8
CHUNKS = 2
BF16 = jnp.bfloat16
F32 = jnp.float32


def rotary_tables(positions_total):
    half = HEAD_SIZE // 2
    frequency = np.exp(np.arange(half) * (-2.0 * math.log(10000.0) / HEAD_SIZE))
    angles = np.arange(positions_total)[:, None] * frequency[None, :]
    cos, sin = np.cos(angles), np.sin(angles)
    return (
        np.concatenate([cos, cos], axis=1).astype(np.float32),
        np.concatenate([-sin, sin], axis=1).astype(np.float32),
    )


def repeat(start, stop, body):
    if stop - start <= 4:
        for i in range(start, stop):
            body(i)
    else:

        def step(i, carry):
            body(i)
            return carry

        lax.fori_loop(start, stop, step, 0)


def dot_nt(a, b):
    return lax.dot_general(a, b, (((1,), (1,)), ((), ())), preferred_element_type=F32)


def dot_tn(a, b):
    return lax.dot_general(a, b, (((0,), (0,)), ((), ())), preferred_element_type=F32)


def dot_nn(a, b):
    return jnp.dot(a, b, preferred_element_type=F32)


def swap_halves(a):
    half = HEAD_SIZE // 2
    return jnp.concatenate([a[:, half:], a[:, :half]], axis=1)


def kernel(
    G, S, D,
    len_ref, x_ref, q_ref, og_ref, k_ref, v_ref, cos_ref, sin_ref,
    qg_ref, ig_ref, kw_ref, vw_ref,
    wbuf, xbuf, xg, pgg, igs, igr, projected,
    zw_s, zw_r, xw_s, xw_r, yw_s, yw_r, ax_s, ax_r, by_s, by_r,
    xs_s, xs_r, zx_s, zx_r, xx_s, xx_r, cx_s, cx_r,
    zp_s, zp_r, xp_s, xp_r, ig_s, ig_r,
):
    g, s, d, c = (lax.axis_index(a) for a in ("groups", "section", "dp", "sub"))
    T = x_ref.shape[1]
    C = k_ref.shape[1]
    R = k_ref.shape[0]
    H = S // 2
    rq = R // (G * D)
    th = T // 2
    kv = C // HEAD_SIZE
    score_scale = HEAD_SIZE ** (-0.5)

    def other_s(k):
        return lax.rem(s + k, S)

    def other_d(k):
        return lax.rem(d + k, D)

    def other_g(k):
        return lax.rem(g + k, G)

    sibling = {"sub": 1 - c}

    def rows_of(gg, dd):
        return pl.ds(pl.multiple_of((gg * D + dd) * rq, rq), rq)

    my_tokens = pl.ds(pl.multiple_of(c * th, th), th)

    def remote(src, dst, send, recv, device):
        return pltpu.make_async_remote_copy(
            src_ref=src, dst_ref=dst, send_sem=send, recv_sem=recv,
            device_id=device, device_id_type=pl.DeviceIdType.MESH,
        )

    def w_z(to, way, block, half):
        part = wbuf.at[block, half, rows_of(g, d)]
        return remote(part, part, zw_s.at[way, block, half], zw_r.at[block, half], {"section": to})

    def w_x(to, block, dd, half):
        part = wbuf.at[block, half, rows_of(g, dd)]
        return remote(part, part, xw_s.at[block, to, half], xw_r.at[block, dd, half], {"dp": to})

    def w_y(to, block, gg, half):
        part = wbuf.at[block, half, rows_of(gg, d)]
        return remote(part, part, yw_s.at[block, to, half], yw_r.at[block, gg, half], {"groups": to})

    def w_ax(to, block, gg, dd, half):
        part = wbuf.at[block, half, rows_of(gg, dd)]
        return remote(part, part, ax_s.at[block, gg, to, half], ax_r.at[block, gg, dd, half], {"dp": to})

    def w_by(to, block, gg, dd, half):
        part = wbuf.at[block, half, rows_of(gg, dd)]
        return remote(part, part, by_s.at[block, to, dd, half], by_r.at[block, gg, dd, half], {"groups": to})

    def x_sub(cc):
        part = xbuf.at[pl.ds(cc * H, H)]
        return remote(part, part, xs_s.at[0], xs_r.at[0], sibling)

    def x_z(to, owner):
        src = xbuf.at[to, my_tokens]
        dst = xg.at[owner, d, my_tokens]
        return remote(src, dst, zx_s.at[to], zx_r.at[owner], {"section": to})

    def x_x(to, block, dd):
        part = xg.at[block, dd, my_tokens]
        return remote(part, part, xx_s.at[block, to], xx_r.at[block, dd], {"dp": to})

    def x_c(cc):
        part = xg.at[:, :, pl.ds(pl.multiple_of(cc * th, th), th)]
        return remote(part, part, cx_s.at[0], cx_r.at[0], sibling)

    def p_z(to, way, owner, h):
        part = pgg.at[owner, d, h]
        return remote(part, part, zp_s.at[way, owner, h], zp_r.at[owner, h], {"section": to})

    def p_x(to, block, dd, h):
        part = pgg.at[block, dd, h]
        return remote(part, part, xp_s.at[block, to, h], xp_r.at[block, dd, h], {"dp": to})

    def i_c(i):
        return remote(igs.at[i], igr.at[i], ig_s.at[i], ig_r.at[i], sibling)

    barrier = pltpu.get_barrier_semaphore()

    def greet(device):
        pl.semaphore_signal(
            barrier, inc=1, device_id=device, device_id_type=pl.DeviceIdType.MESH
        )

    greet(sibling)
    repeat(1, S, lambda k: greet({"section": other_s(k)}))
    repeat(1, D, lambda k: greet({"dp": other_d(k)}))
    repeat(1, G, lambda k: greet({"groups": other_g(k)}))
    wbuf[s, 0] = k_ref[...]
    wbuf[s, 1] = v_ref[...]
    for i in range(H):
        xbuf[c * H + i] = x_ref[0, :, i * R : (i + 1) * R]
    pl.semaphore_wait(barrier, 1 + (S - 1) + (D - 1) + (G - 1))

    def along_line(k, body):
        @pl.when(s >= k)
        def _():
            body(s - k, 0, s < S - 1, s + 1)

        @pl.when(s + k < S)
        def _():
            body(s + k, 1, s > 0, s - 1)

    def both_ways(body):
        @pl.when(s < S - 1)
        def _():
            body(s + 1, 0)

        @pl.when(s > 0)
        def _():
            body(s - 1, 1)

    x_sub(c).start()
    for half in range(CHUNKS):
        both_ways(lambda to, way: w_z(to, way, s, half).start())
    x_sub(1 - c).wait_recv()
    xg[s, d, my_tokens] = xbuf[s, my_tokens]
    repeat(1, D, lambda j: x_x(other_d(j), s, d).start())
    projected[:, :C] = dot_nn(xbuf[s], wbuf[s, 0])
    projected[:, C:] = dot_nn(xbuf[s], wbuf[s, 1])

    def first_hand(block, way, more, to):
        for half in range(CHUNKS):
            w_z(s, way, block, half).wait_recv()

            @pl.when(more)
            def _():
                w_z(to, way, block, half).start()

            repeat(1, G, lambda j: w_y(other_g(j), block, g, half).start())
            repeat(1, D, lambda j: w_x(other_d(j), block, d, half).start())

    def second_hand(block, way, more, to):
        for half in range(CHUNKS):

            def from_y(j):
                gg = other_g(j)
                w_y(gg, block, gg, half).wait_recv()
                if half < CHUNKS // 2:
                    repeat(1, D, lambda i: w_ax(other_d(i), block, gg, d, half).start())

            def from_x(j):
                dd = other_d(j)
                w_x(dd, block, dd, half).wait_recv()
                if half >= CHUNKS // 2:
                    repeat(1, G, lambda i: w_by(other_g(i), block, g, dd, half).start())

            repeat(1, G, from_y)
            repeat(1, D, from_x)

    def project(block, way, more, to):
        def diagonal(j):
            gg = other_g(j)

            def part(i):
                dd = other_d(i)
                for half in range(CHUNKS // 2):
                    w_ax(dd, block, gg, dd, half).wait_recv()
                for half in range(CHUNKS // 2, CHUNKS):
                    w_by(gg, block, gg, dd, half).wait_recv()

            repeat(1, D, part)

        repeat(1, G, diagonal)
        projected[:, :C] += dot_nn(xbuf[block], wbuf[block, 0])
        projected[:, C:] += dot_nn(xbuf[block], wbuf[block, 1])

    along_line(1, first_hand)

    def hop(k):
        along_line(k, first_hand)
        along_line(k - 1, second_hand)

    repeat(2, S, hop)
    repeat(1, S, lambda k: x_z(other_s(k), s).start())
    along_line(S - 1, second_hand)

    def inputs_on(k):
        block = other_s(k)
        x_z(block, block).wait_recv()
        repeat(1, D, lambda j: x_x(other_d(j), block, d).start())

    repeat(1, S, lambda k: along_line(k, project))
    repeat(1, S, inputs_on)

    cos, sin = cos_ref[...], sin_ref[...]
    length = len_ref[0]
    u_ids = lax.broadcasted_iota(jnp.int32, (T, T), 0)
    t_ids = lax.broadcasted_iota(jnp.int32, (T, T), 1)
    allowed = (u_ids <= t_ids) & (u_ids < length)
    for h in range(kv):
        linear = projected[:, h * HEAD_SIZE : (h + 1) * HEAD_SIZE]
        keys = (linear * cos + swap_halves(linear) * sin).astype(BF16)
        values = projected[:, C + h * HEAD_SIZE : C + (h + 1) * HEAD_SIZE].astype(BF16)
        key_grad = jnp.zeros((T, HEAD_SIZE), F32)
        value_grad = jnp.zeros((T, HEAD_SIZE), F32)
        for j in range(QUERY_GROUP):
            at = slice((h * QUERY_GROUP + j) * HEAD_SIZE, (h * QUERY_GROUP + j + 1) * HEAD_SIZE)
            query, grad = q_ref[0, :, at], og_ref[0, :, at]
            scores = jnp.where(allowed, dot_nt(keys, query) * score_scale, -1e30)
            exponent = jnp.exp(scores - jnp.max(scores, axis=0, keepdims=True))
            probs = exponent / jnp.sum(exponent, axis=0, keepdims=True)
            prob_grad = dot_nt(values, grad)
            centre = jnp.sum(probs * prob_grad, axis=0, keepdims=True)
            logit_grad = (probs * (prob_grad - centre) * score_scale).astype(BF16)
            qg_ref[0, :, at] = dot_tn(logit_grad, keys).astype(BF16)
            key_grad += dot_nn(logit_grad, query)
            value_grad += dot_nn(probs.astype(BF16), grad)
        key_grad = key_grad * cos - swap_halves(key_grad) * sin
        pgg[s, d, h, :, :HEAD_SIZE] = key_grad.astype(BF16)
        pgg[s, d, h, :, HEAD_SIZE:] = value_grad.astype(BF16)
        both_ways(lambda to, way: p_z(to, way, s, h).start())
        repeat(1, D, lambda j: p_x(other_d(j), s, d, h).start())

    def by_matrix(parts):
        return jnp.concatenate(
            [p[:, :HEAD_SIZE] for p in parts] + [p[:, HEAD_SIZE:] for p in parts], axis=1
        )

    proj_grads = by_matrix([pgg[s, d, h] for h in range(kv)])

    def input_part(block):
        return dot_nt(proj_grads[:, :C], wbuf[block, 0]) + dot_nt(proj_grads[:, C:], wbuf[block, 1])

    for i in range(H):
        igs[i] = input_part((1 - c) * H + i)
        i_c(i).start()

    def grads_on(block, way, more, to):
        for h in range(kv):
            p_z(s, way, block, h).wait_recv()

            @pl.when(more)
            def _():
                p_z(to, way, block, h).start()

            repeat(1, D, lambda j: p_x(other_d(j), block, d, h).start())

    repeat(1, S, lambda k: along_line(k, grads_on))

    def inputs_in(block):
        def part(j):
            dd = other_d(j)
            x_x(dd, block, dd).wait_recv()

        repeat(1, D, part)

    repeat(0, S, inputs_in)
    x_c(c).start()
    for i in range(H):
        own = input_part(c * H + i)
        i_c(i).wait_recv()
        ig_ref[0, :, i * R : (i + 1) * R] = (own + igr[i]).astype(BF16)

    x_c(1 - c).wait_recv()

    def grads_in(block):
        def part(j):
            dd = other_d(j)
            for h in range(kv):
                p_x(dd, block, dd, h).wait_recv()

        repeat(1, D, part)

    repeat(0, S, grads_in)

    mean = 1.0 / (S * D)
    tile = min(R, 256)
    if S * D * T <= 1024:
        for h in range(kv):
            at = slice(h * HEAD_SIZE, (h + 1) * HEAD_SIZE)
            ps = pgg[:, :, h].reshape(S * D * T, 2 * HEAD_SIZE)
            for r in range(0, R, tile):
                xs = xg[:, :, :, r : r + tile].reshape(S * D * T, tile)
                part = dot_tn(xs, ps) * mean
                kw_ref[r : r + tile, at] = part[:, :HEAD_SIZE]
                vw_ref[r : r + tile, at] = part[:, HEAD_SIZE:]
    else:
        kw_ref[...] = jnp.zeros_like(kw_ref)
        vw_ref[...] = jnp.zeros_like(vw_ref)

        def add_batch(b, carry):
            for h in range(kv):
                at = slice(h * HEAD_SIZE, (h + 1) * HEAD_SIZE)
                part = dot_tn(xg[b // D, lax.rem(b, D)], pgg[b // D, lax.rem(b, D), h]) * mean
                kw_ref[:, at] += part[:, :HEAD_SIZE]
                vw_ref[:, at] += part[:, HEAD_SIZE:]
            return carry

        lax.fori_loop(0, S * D, add_batch, 0)

    x_sub(c).wait_send()
    x_c(c).wait_send()
    for i in range(H):
        i_c(i).wait_send()
    repeat(1, D, lambda j: x_x(other_d(j), s, d).wait_send())
    for h in range(kv):
        repeat(1, D, lambda j: p_x(other_d(j), s, d, h).wait_send())

    def line_sent(to, way, block):
        for half in range(CHUNKS):
            w_z(to, way, block, half).wait_send()
        for h in range(kv):
            p_z(to, way, block, h).wait_send()

    both_ways(lambda to, way: line_sent(to, way, s))

    def sent(block, way, more, to):
        @pl.when(more)
        def _():
            line_sent(to, way, block)

        x_z(block, s).wait_send()

        def along_y(j):
            gg = other_g(j)
            for half in range(CHUNKS):
                w_y(gg, block, g, half).wait_send()

            def both(i):
                dd = other_d(i)
                for half in range(CHUNKS // 2):
                    w_ax(dd, block, gg, d, half).wait_send()
                for half in range(CHUNKS // 2, CHUNKS):
                    w_by(gg, block, g, dd, half).wait_send()

            repeat(1, D, both)

        def along_x(j):
            dd = other_d(j)
            for half in range(CHUNKS):
                w_x(dd, block, d, half).wait_send()
            x_x(dd, block, d).wait_send()
            for h in range(kv):
                p_x(dd, block, d, h).wait_send()

        repeat(1, G, along_y)
        repeat(1, D, along_x)

    repeat(1, S, lambda k: along_line(k, sent))


def hand_out(*refs):
    ins, outs, held, sems = refs[:4], refs[4:8], refs[8:12], refs[12]
    loads = [pltpu.make_async_copy(ins[i], held[i], sems.at[0, i]) for i in range(4)]
    stores = [pltpu.make_async_copy(held[i], outs[i], sems.at[1, i]) for i in range(4)]
    for load in loads:
        load.start()
    for load, store in zip(loads, stores):
        load.wait()
        store.start()
    for store in stores:
        store.wait()


def shards(G, S, D, inputs, queries, out_grad, lengths, key_matrix, value_matrix):
    T = inputs.shape[1]
    R, C = key_matrix.shape
    H = S // 2
    kv = C // HEAD_SIZE
    cos, sin = rotary_tables(T)
    dma = pltpu.SemaphoreType.DMA
    vmem = pl.BlockSpec(memory_space=pltpu.VMEM)
    pairs = lambda *shape: [dma(shape), dma(shape)]
    results = pl.pallas_call(
        functools.partial(kernel, G, S, D),
        out_shape=(
            jax.ShapeDtypeStruct(queries.shape, BF16),
            jax.ShapeDtypeStruct(inputs.shape, BF16),
            jax.ShapeDtypeStruct((R, C), F32),
            jax.ShapeDtypeStruct((R, C), F32),
        ),
        in_specs=[pl.BlockSpec(memory_space=pltpu.SMEM)] + [vmem] * 7,
        out_specs=(vmem,) * 4,
        scratch_shapes=[
            pltpu.VMEM((S, CHUNKS, R, C), BF16),
            pltpu.VMEM((S, T, R), BF16),
            pltpu.VMEM((S, D, T, R), BF16),
            pltpu.VMEM((S, D, kv, T, 2 * HEAD_SIZE), BF16),
            pltpu.VMEM((H, T, R), F32),
            pltpu.VMEM((H, T, R), F32),
            pltpu.VMEM((T, 2 * C), F32),
            dma((2, S, CHUNKS)), dma((S, CHUNKS)), *pairs(S, D, CHUNKS), *pairs(S, G, CHUNKS),
            *pairs(S, G, D, CHUNKS), *pairs(S, G, D, CHUNKS),
            *pairs(1), *pairs(S), *pairs(S, D), *pairs(1),
            dma((2, S, kv)), dma((S, kv)), *pairs(S, D, kv), *pairs(H),
        ],
        compiler_params=pltpu.CompilerParams(
            collective_id=0, has_side_effects=True, vmem_limit_bytes=56 * 2**20
        ),
    )(lengths, inputs, queries, out_grad, key_matrix, value_matrix, jnp.asarray(cos), jnp.asarray(sin))
    anywhere = pl.BlockSpec(memory_space=pl.ANY)
    return pl.pallas_call(
        hand_out,
        out_shape=tuple(jax.ShapeDtypeStruct(r.shape, r.dtype) for r in results),
        in_specs=[anywhere] * 4,
        out_specs=(anywhere,) * 4,
        scratch_shapes=[*(pltpu.VMEM(r.shape, r.dtype) for r in results), dma((2, 4))],
    )(*results)


def solution(mesh):
    sizes = (mesh.shape["groups"], mesh.shape["section"], mesh.shape["dp"])
    batch = P(("groups", "section", "dp"), None, "sub")
    weights = P("section", "sub")
    rows = P(("groups", "section"), "sub")
    return jax.shard_map(
        functools.partial(shards, *sizes),
        mesh=mesh,
        in_specs=(batch, batch, batch, P(("groups", "section", "dp")), weights, weights),
        out_specs=(batch, batch, rows, rows),
        check_vma=False,
    )
```

```python
import functools
import math

import jax
import jax.numpy as jnp
import numpy as np
from jax import lax
from jax.experimental import pallas as pl
from jax.experimental.pallas import tpu as pltpu
from jax.sharding import PartitionSpec as P

HEAD_SIZE = 128
QUERY_GROUP = 8
CHUNKS = 2
BF16 = jnp.bfloat16
F32 = jnp.float32


def rotary_tables(positions_total):
    half = HEAD_SIZE // 2
    frequency = np.exp(np.arange(half) * (-2.0 * math.log(10000.0) / HEAD_SIZE))
    angles = np.arange(positions_total)[:, None] * frequency[None, :]
    cos, sin = np.cos(angles), np.sin(angles)
    return (
        np.concatenate([cos, cos], axis=1).astype(np.float32),
        np.concatenate([-sin, sin], axis=1).astype(np.float32),
    )


def repeat(start, stop, body):
    if stop - start <= 4:
        for i in range(start, stop):
            body(i)
    else:

        def step(i, carry):
            body(i)
            return carry

        lax.fori_loop(start, stop, step, 0)


def dot_nt(a, b):
    return lax.dot_general(a, b, (((1,), (1,)), ((), ())), preferred_element_type=F32)


def dot_tn(a, b):
    return lax.dot_general(a, b, (((0,), (0,)), ((), ())), preferred_element_type=F32)


def dot_nn(a, b):
    return jnp.dot(a, b, preferred_element_type=F32)


def swap_halves(a):
    half = HEAD_SIZE // 2
    return jnp.concatenate([a[:, half:], a[:, :half]], axis=1)


def kernel(
    G, S, D,
    len_ref, x_ref, q_ref, og_ref, k_ref, v_ref, cos_ref, sin_ref,
    qg_ref, ig_ref, kw_ref, vw_ref,
    wbuf, xbuf, xg, pgg, igs, igr, projected, q_buf, og_buf, ld,
    zw_s, zw_r, xw_s, xw_r, yw_s, yw_r, ax_s, ax_r, by_s, by_r,
    xs_s, xs_r, zx_s, zx_r, xx_s, xx_r, cx_s, cx_r,
    zp_s, zp_r, xp_s, xp_r, ig_s, ig_r,
):
    g, s, d, c = (lax.axis_index(a) for a in ("groups", "section", "dp", "sub"))
    T = x_ref.shape[1]
    C = k_ref.shape[1]
    R = k_ref.shape[0]
    H = S // 2
    rq = R // (G * D)
    th = T // 2
    kv = C // HEAD_SIZE
    score_scale = HEAD_SIZE ** (-0.5)

    def other_s(k):
        return lax.rem(s + k, S)

    def other_d(k):
        return lax.rem(d + k, D)

    def other_g(k):
        return lax.rem(g + k, G)

    sibling = {"sub": 1 - c}

    def rows_of(gg, dd):
        return pl.ds(pl.multiple_of((gg * D + dd) * rq, rq), rq)

    my_tokens = pl.ds(pl.multiple_of(c * th, th), th)

    def remote(src, dst, send, recv, device):
        return pltpu.make_async_remote_copy(
            src_ref=src, dst_ref=dst, send_sem=send, recv_sem=recv,
            device_id=device, device_id_type=pl.DeviceIdType.MESH,
        )

    def w_z(to, way, block, half):
        part = wbuf.at[block, half, rows_of(g, d)]
        return remote(part, part, zw_s.at[way, block, half], zw_r.at[block, half], {"section": to})

    def w_x(to, block, dd, half):
        part = wbuf.at[block, half, rows_of(g, dd)]
        return remote(part, part, xw_s.at[block, to, half], xw_r.at[block, dd, half], {"dp": to})

    def w_y(to, block, gg, half):
        part = wbuf.at[block, half, rows_of(gg, d)]
        return remote(part, part, yw_s.at[block, to, half], yw_r.at[block, gg, half], {"groups": to})

    def w_ax(to, block, gg, dd, half):
        part = wbuf.at[block, half, rows_of(gg, dd)]
        return remote(part, part, ax_s.at[block, gg, to, half], ax_r.at[block, gg, dd, half], {"dp": to})

    def w_by(to, block, gg, dd, half):
        part = wbuf.at[block, half, rows_of(gg, dd)]
        return remote(part, part, by_s.at[block, to, dd, half], by_r.at[block, gg, dd, half], {"groups": to})

    def x_sub(cc):
        part = xbuf.at[pl.ds(cc * H, H)]
        return remote(part, part, xs_s.at[0], xs_r.at[0], sibling)

    def x_z(to, owner):
        src = xbuf.at[to, my_tokens]
        dst = xg.at[owner, d, my_tokens]
        return remote(src, dst, zx_s.at[to], zx_r.at[owner], {"section": to})

    def x_x(to, block, dd):
        part = xg.at[block, dd, my_tokens]
        return remote(part, part, xx_s.at[block, to], xx_r.at[block, dd], {"dp": to})

    def x_c(cc):
        part = xg.at[:, :, pl.ds(pl.multiple_of(cc * th, th), th)]
        return remote(part, part, cx_s.at[0], cx_r.at[0], sibling)

    def p_z(to, way, owner, h):
        part = pgg.at[owner, d, h]
        return remote(part, part, zp_s.at[way, owner, h], zp_r.at[owner, h], {"section": to})

    def p_x(to, block, dd, h):
        part = pgg.at[block, dd, h]
        return remote(part, part, xp_s.at[block, to, h], xp_r.at[block, dd, h], {"dp": to})

    def i_c(i):
        return remote(igs.at[i], igr.at[i], ig_s.at[i], ig_r.at[i], sibling)

    barrier = pltpu.get_barrier_semaphore()

    def greet(device):
        pl.semaphore_signal(
            barrier, inc=1, device_id=device, device_id_type=pl.DeviceIdType.MESH
        )

    greet(sibling)
    repeat(1, S, lambda k: greet({"section": other_s(k)}))
    repeat(1, D, lambda k: greet({"dp": other_d(k)}))
    repeat(1, G, lambda k: greet({"groups": other_g(k)}))
    load = pltpu.make_async_copy
    weights_in = [load(r, wbuf.at[s, i], ld.at[i]) for i, r in enumerate((k_ref, v_ref))]
    inputs_here = [
        load(x_ref.at[0, :, pl.ds(i * R, R)], xbuf.at[c * H + i], ld.at[2 + i]) for i in range(H)
    ]
    heads_in = [load(r, b, ld.at[2 + H + i]) for i, (r, b) in enumerate(((q_ref, q_buf), (og_ref, og_buf)))]
    for copy in weights_in + inputs_here + heads_in:
        copy.start()
    for copy in weights_in:
        copy.wait()
    pl.semaphore_wait(barrier, 1 + (S - 1) + (D - 1) + (G - 1))

    def along_line(k, body):
        @pl.when(s >= k)
        def _():
            body(s - k, 0, s < S - 1, s + 1)

        @pl.when(s + k < S)
        def _():
            body(s + k, 1, s > 0, s - 1)

    def both_ways(body):
        @pl.when(s < S - 1)
        def _():
            body(s + 1, 0)

        @pl.when(s > 0)
        def _():
            body(s - 1, 1)

    for half in range(CHUNKS):
        both_ways(lambda to, way: w_z(to, way, s, half).start())
    for copy in inputs_here:
        copy.wait()
    x_sub(c).start()
    x_sub(1 - c).wait_recv()
    xg[s, d, my_tokens] = xbuf[s, my_tokens]
    repeat(1, D, lambda j: x_x(other_d(j), s, d).start())
    projected[:, :C] = dot_nn(xbuf[s], wbuf[s, 0])
    projected[:, C:] = dot_nn(xbuf[s], wbuf[s, 1])

    def first_hand(block, way, more, to):
        for half in range(CHUNKS):
            w_z(s, way, block, half).wait_recv()

            @pl.when(more)
            def _():
                w_z(to, way, block, half).start()

            repeat(1, G, lambda j: w_y(other_g(j), block, g, half).start())
            repeat(1, D, lambda j: w_x(other_d(j), block, d, half).start())

    def second_hand(block, way, more, to):
        for half in range(CHUNKS):

            def from_y(j):
                gg = other_g(j)
                w_y(gg, block, gg, half).wait_recv()
                if half < CHUNKS // 2:
                    repeat(1, D, lambda i: w_ax(other_d(i), block, gg, d, half).start())

            def from_x(j):
                dd = other_d(j)
                w_x(dd, block, dd, half).wait_recv()
                if half >= CHUNKS // 2:
                    repeat(1, G, lambda i: w_by(other_g(i), block, g, dd, half).start())

            repeat(1, G, from_y)
            repeat(1, D, from_x)

    def project(block, way, more, to):
        def diagonal(j):
            gg = other_g(j)

            def part(i):
                dd = other_d(i)
                for half in range(CHUNKS // 2):
                    w_ax(dd, block, gg, dd, half).wait_recv()
                for half in range(CHUNKS // 2, CHUNKS):
                    w_by(gg, block, gg, dd, half).wait_recv()

            repeat(1, D, part)

        repeat(1, G, diagonal)
        projected[:, :C] += dot_nn(xbuf[block], wbuf[block, 0])
        projected[:, C:] += dot_nn(xbuf[block], wbuf[block, 1])

    along_line(1, first_hand)

    def hop(k):
        along_line(k, first_hand)
        along_line(k - 1, second_hand)

    repeat(2, S, hop)
    repeat(1, S, lambda k: x_z(other_s(k), s).start())
    along_line(S - 1, second_hand)

    def inputs_on(k):
        block = other_s(k)
        x_z(block, block).wait_recv()
        repeat(1, D, lambda j: x_x(other_d(j), block, d).start())

    repeat(1, S, lambda k: along_line(k, project))
    repeat(1, S, inputs_on)

    for copy in heads_in:
        copy.wait()
    cos, sin = cos_ref[...], sin_ref[...]
    length = len_ref[0]
    u_ids = lax.broadcasted_iota(jnp.int32, (T, T), 0)
    t_ids = lax.broadcasted_iota(jnp.int32, (T, T), 1)
    allowed = (u_ids <= t_ids) & (u_ids < length)
    for h in range(kv):
        linear = projected[:, h * HEAD_SIZE : (h + 1) * HEAD_SIZE]
        keys = (linear * cos + swap_halves(linear) * sin).astype(BF16)
        values = projected[:, C + h * HEAD_SIZE : C + (h + 1) * HEAD_SIZE].astype(BF16)
        key_grad = jnp.zeros((T, HEAD_SIZE), F32)
        value_grad = jnp.zeros((T, HEAD_SIZE), F32)
        for j in range(QUERY_GROUP):
            at = slice((h * QUERY_GROUP + j) * HEAD_SIZE, (h * QUERY_GROUP + j + 1) * HEAD_SIZE)
            query, grad = q_buf[0, :, at], og_buf[0, :, at]
            scores = jnp.where(allowed, dot_nt(keys, query) * score_scale, -1e30)
            exponent = jnp.exp(scores - jnp.max(scores, axis=0, keepdims=True))
            probs = exponent / jnp.sum(exponent, axis=0, keepdims=True)
            prob_grad = dot_nt(values, grad)
            centre = jnp.sum(probs * prob_grad, axis=0, keepdims=True)
            logit_grad = (probs * (prob_grad - centre) * score_scale).astype(BF16)
            qg_ref[0, :, at] = dot_tn(logit_grad, keys).astype(BF16)
            key_grad += dot_nn(logit_grad, query)
            value_grad += dot_nn(probs.astype(BF16), grad)
        key_grad = key_grad * cos - swap_halves(key_grad) * sin
        pgg[s, d, h, :, :HEAD_SIZE] = key_grad.astype(BF16)
        pgg[s, d, h, :, HEAD_SIZE:] = value_grad.astype(BF16)
        both_ways(lambda to, way: p_z(to, way, s, h).start())
        repeat(1, D, lambda j: p_x(other_d(j), s, d, h).start())

    def by_matrix(parts):
        return jnp.concatenate(
            [p[:, :HEAD_SIZE] for p in parts] + [p[:, HEAD_SIZE:] for p in parts], axis=1
        )

    proj_grads = by_matrix([pgg[s, d, h] for h in range(kv)])

    def input_part(block):
        return dot_nt(proj_grads[:, :C], wbuf[block, 0]) + dot_nt(proj_grads[:, C:], wbuf[block, 1])

    for i in range(H):
        igs[i] = input_part((1 - c) * H + i)
        i_c(i).start()

    def grads_on(block, way, more, to):
        for h in range(kv):
            p_z(s, way, block, h).wait_recv()

            @pl.when(more)
            def _():
                p_z(to, way, block, h).start()

            repeat(1, D, lambda j: p_x(other_d(j), block, d, h).start())

    repeat(1, S, lambda k: along_line(k, grads_on))

    def inputs_in(block):
        def part(j):
            dd = other_d(j)
            x_x(dd, block, dd).wait_recv()

        repeat(1, D, part)

    repeat(0, S, inputs_in)
    x_c(c).start()
    for i in range(H):
        own = input_part(c * H + i)
        i_c(i).wait_recv()
        ig_ref[0, :, i * R : (i + 1) * R] = (own + igr[i]).astype(BF16)

    x_c(1 - c).wait_recv()

    def grads_in(block):
        def part(j):
            dd = other_d(j)
            for h in range(kv):
                p_x(dd, block, dd, h).wait_recv()

        repeat(1, D, part)

    repeat(0, S, grads_in)

    mean = 1.0 / (S * D)
    tile = min(R, 256)
    if S * D * T <= 1024:
        for h in range(kv):
            at = slice(h * HEAD_SIZE, (h + 1) * HEAD_SIZE)
            ps = pgg[:, :, h].reshape(S * D * T, 2 * HEAD_SIZE)
            for r in range(0, R, tile):
                xs = xg[:, :, :, r : r + tile].reshape(S * D * T, tile)
                part = dot_tn(xs, ps) * mean
                kw_ref[r : r + tile, at] = part[:, :HEAD_SIZE]
                vw_ref[r : r + tile, at] = part[:, HEAD_SIZE:]
    else:
        kw_ref[...] = jnp.zeros_like(kw_ref)
        vw_ref[...] = jnp.zeros_like(vw_ref)

        def add_batch(b, carry):
            for h in range(kv):
                at = slice(h * HEAD_SIZE, (h + 1) * HEAD_SIZE)
                part = dot_tn(xg[b // D, lax.rem(b, D)], pgg[b // D, lax.rem(b, D), h]) * mean
                kw_ref[:, at] += part[:, :HEAD_SIZE]
                vw_ref[:, at] += part[:, HEAD_SIZE:]
            return carry

        lax.fori_loop(0, S * D, add_batch, 0)

    x_sub(c).wait_send()
    x_c(c).wait_send()
    for i in range(H):
        i_c(i).wait_send()
    repeat(1, D, lambda j: x_x(other_d(j), s, d).wait_send())
    for h in range(kv):
        repeat(1, D, lambda j: p_x(other_d(j), s, d, h).wait_send())

    def line_sent(to, way, block):
        for half in range(CHUNKS):
            w_z(to, way, block, half).wait_send()
        for h in range(kv):
            p_z(to, way, block, h).wait_send()

    both_ways(lambda to, way: line_sent(to, way, s))

    def sent(block, way, more, to):
        @pl.when(more)
        def _():
            line_sent(to, way, block)

        x_z(block, s).wait_send()

        def along_y(j):
            gg = other_g(j)
            for half in range(CHUNKS):
                w_y(gg, block, g, half).wait_send()

            def both(i):
                dd = other_d(i)
                for half in range(CHUNKS // 2):
                    w_ax(dd, block, gg, d, half).wait_send()
                for half in range(CHUNKS // 2, CHUNKS):
                    w_by(gg, block, g, dd, half).wait_send()

            repeat(1, D, both)

        def along_x(j):
            dd = other_d(j)
            for half in range(CHUNKS):
                w_x(dd, block, d, half).wait_send()
            x_x(dd, block, d).wait_send()
            for h in range(kv):
                p_x(dd, block, d, h).wait_send()

        repeat(1, G, along_y)
        repeat(1, D, along_x)

    repeat(1, S, lambda k: along_line(k, sent))


def hand_out(*refs):
    ins, outs, held, sems = refs[:4], refs[4:8], refs[8:12], refs[12]
    loads = [pltpu.make_async_copy(ins[i], held[i], sems.at[0, i]) for i in range(4)]
    stores = [pltpu.make_async_copy(held[i], outs[i], sems.at[1, i]) for i in range(4)]
    for load in loads:
        load.start()
    for load, store in zip(loads, stores):
        load.wait()
        store.start()
    for store in stores:
        store.wait()


def shards(G, S, D, inputs, queries, out_grad, lengths, key_matrix, value_matrix):
    T = inputs.shape[1]
    R, C = key_matrix.shape
    H = S // 2
    kv = C // HEAD_SIZE
    cos, sin = rotary_tables(T)
    dma = pltpu.SemaphoreType.DMA
    vmem = pl.BlockSpec(memory_space=pltpu.VMEM)
    pairs = lambda *shape: [dma(shape), dma(shape)]
    results = pl.pallas_call(
        functools.partial(kernel, G, S, D),
        out_shape=(
            jax.ShapeDtypeStruct(queries.shape, BF16),
            jax.ShapeDtypeStruct(inputs.shape, BF16),
            jax.ShapeDtypeStruct((R, C), F32),
            jax.ShapeDtypeStruct((R, C), F32),
        ),
        in_specs=[pl.BlockSpec(memory_space=pltpu.SMEM)] + [pl.BlockSpec(memory_space=pl.ANY)] * 5 + [vmem] * 2,
        out_specs=(vmem,) * 4,
        scratch_shapes=[
            pltpu.VMEM((S, CHUNKS, R, C), BF16),
            pltpu.VMEM((S, T, R), BF16),
            pltpu.VMEM((S, D, T, R), BF16),
            pltpu.VMEM((S, D, kv, T, 2 * HEAD_SIZE), BF16),
            pltpu.VMEM((H, T, R), F32),
            pltpu.VMEM((H, T, R), F32),
            pltpu.VMEM((T, 2 * C), F32),
            pltpu.VMEM(queries.shape, BF16),
            pltpu.VMEM(queries.shape, BF16),
            dma((4 + H,)),
            dma((2, S, CHUNKS)), dma((S, CHUNKS)), *pairs(S, D, CHUNKS), *pairs(S, G, CHUNKS),
            *pairs(S, G, D, CHUNKS), *pairs(S, G, D, CHUNKS),
            *pairs(1), *pairs(S), *pairs(S, D), *pairs(1),
            dma((2, S, kv)), dma((S, kv)), *pairs(S, D, kv), *pairs(H),
        ],
        compiler_params=pltpu.CompilerParams(
            collective_id=0, has_side_effects=True, vmem_limit_bytes=56 * 2**20
        ),
    )(lengths, inputs, queries, out_grad, key_matrix, value_matrix, jnp.asarray(cos), jnp.asarray(sin))
    anywhere = pl.BlockSpec(memory_space=pl.ANY)
    return pl.pallas_call(
        hand_out,
        out_shape=tuple(jax.ShapeDtypeStruct(r.shape, r.dtype) for r in results),
        in_specs=[anywhere] * 4,
        out_specs=(anywhere,) * 4,
        scratch_shapes=[*(pltpu.VMEM(r.shape, r.dtype) for r in results), dma((2, 4))],
    )(*results)


def solution(mesh):
    sizes = (mesh.shape["groups"], mesh.shape["section"], mesh.shape["dp"])
    batch = P(("groups", "section", "dp"), None, "sub")
    weights = P("section", "sub")
    rows = P(("groups", "section"), "sub")
    return jax.shard_map(
        functools.partial(shards, *sizes),
        mesh=mesh,
        in_specs=(batch, batch, batch, P(("groups", "section", "dp")), weights, weights),
        out_specs=(batch, batch, rows, rows),
        check_vma=False,
    )
```
